512 devices in a mesh: hst: 64 (over z, x, core), tensor: 8 (over y).
Axes of the slice: x: 4, y: 8, z: 8, core: 2. Of those that a mesh axis runs over, the one named last changes fastest.
Arguments:
- queries: bfloat16 [12288, 8192], P('hst', 'tensor'), may hold values from -11 to 11
- keys: bfloat16 [12288, 1024], P('hst', 'tensor'), may hold values from -6.5 to 6.5
- values: bfloat16 [12288, 1024], P('hst', 'tensor'), may hold values from -6 to 6
- keep_index: int32 [64, 8, 128], P('hst', 'tensor'), may hold values from 0 to 191, as said below
- keep_count: int32 [64, 8, 1], P('hst', 'tensor'), may hold values from 32 to 96, as said below
Outputs:
- attended: bfloat16 [12288, 8192], P(('hst', 'tensor'))
The draws below stay inside these ranges and needn't reach their ends.
Inputs may be any that keep to these rules, and one draw needn't show every extreme that they name: `keep_index`: a row within the host block of 192 rows. `keep_count`: slots of a block at or past its count are padding.
All inputs are finite; a program needn't handle non-finite values.
Results may differ from the reference program's by a relative error of at most 0.0065.
Values may be sent and summed in bfloat16 or wider, within the bound.
No kernel may reach another device: no remote copies, remote signals or barrier semaphores. Data moves between devices by JAX's collectives and lax.ppermute only.
A program may use at most 64 MiB of HBM per device.

```python
import jax
import jax.numpy as jnp
from jax import lax

QH = 64
KVH = 8
HD = 128
TOK_DEV = 192
ANCHOR = 128
BLOCK = 128
KBLOCKS = 1
KEEP = 128
TOKENS = 12288


def draw_queries(key, part):
    key = jax.random.fold_in(key, 11)
    first_key = jax.random.fold_in(key, 0)
    return jnp.clip(1.5 * jax.random.normal(first_key, (TOKENS, QH * HD), jnp.float32), -6.0, 6.0).astype(jnp.bfloat16)


def draw_keys(key, part):
    key = jax.random.fold_in(key, 12)
    return jnp.clip(jax.random.normal(key, (TOKENS, KVH * HD), jnp.float32), -5.0, 5.0).astype(jnp.bfloat16)


def draw_keep_index(key, part):
    key = jax.random.fold_in(key, 13)
    host_total = TOKENS // TOK_DEV
    list_keys = jax.random.split(key, host_total * KVH)
    lists = jax.vmap(lambda single: jax.random.permutation(single, TOK_DEV)[:KEEP])(list_keys)
    lists = lists.reshape(host_total, KVH, KEEP).astype(jnp.int32)
    lists = lists.at[0, 0, 0].set(TOK_DEV - 1)
    lists = lists.at[0, 0, 1].set(0)
    return lists


def draw_keep_count(key, part):
    key = jax.random.fold_in(key, 14)
    host_total = TOKENS // TOK_DEV
    first_key, second_key, third_key = jax.random.split(key, 3)
    counts = jax.random.randint(first_key, (host_total * KVH * KBLOCKS,), BLOCK // 4, 3 * BLOCK // 4 + 1, jnp.int32)
    total_cells = host_total * KVH * KBLOCKS
    spot_high = jax.random.randint(second_key, (), 0, total_cells, jnp.int32)
    offset = jax.random.randint(third_key, (), 1, total_cells, jnp.int32)
    spot_low = (spot_high + offset) % total_cells
    counts = counts.at[spot_high].set(3 * BLOCK // 4)
    counts = counts.at[spot_low].set(BLOCK // 4)
    return counts.reshape(host_total, KVH, KBLOCKS)


def level_of(stream_key, shape, cuts, least, high):
    loudness = 1.0
    for axis_at, parts in cuts:
        steps = jax.random.uniform(jax.random.fold_in(jax.random.fold_in(stream_key, 6), axis_at), (parts,), jnp.float32, least / len(cuts), high / len(cuts))
        loudness = loudness * jnp.repeat(jnp.exp(steps), shape[axis_at] // parts).reshape((-1,) + (1,) * (len(shape) - 1 - axis_at))
    return loudness


def centred(own_key, shape, scale, bound, cuts=(), kind=jnp.bfloat16):
    entries = jax.random.normal(own_key, shape, jnp.float32) * scale
    if len(cuts) > 0:
        entries = level_of(own_key, shape, cuts, -0.22, 0.18) * entries
    return jnp.clip(entries, min=-bound, max=bound).astype(kind)


def setup_inputs(seed: int = 0) -> dict:
    key_list = jax.random.split(jax.random.key(seed), 6)
    return {
        "queries": draw_queries(jax.random.fold_in(key_list[5], 71), 0),
        "keys": draw_keys(jax.random.fold_in(key_list[5], 71), 0),
        "values": centred(key_list[2], (TOKENS, KVH * HD), 1.0, 6.0, ((0, 64), (1, 8))),
        "keep_index": draw_keep_index(jax.random.fold_in(key_list[5], 71), 0),
        "keep_count": draw_keep_count(jax.random.fold_in(key_list[5], 71), 0),
    }


def pick_rows(slot_rows, column):
    return column[slot_rows]


def reference(queries, keys, values, keep_index, keep_count):
    host_total = TOKENS // TOK_DEV
    group_size = QH // KVH
    score_scale = HD ** -0.5
    query_rows = queries.reshape(host_total, TOK_DEV, KVH, group_size, HD)
    key_rows = keys.reshape(host_total, TOK_DEV, KVH, HD)
    value_rows = values.reshape(host_total, TOK_DEV, KVH, HD)
    picker = jax.vmap(jax.vmap(pick_rows, in_axes=(0, 1)))
    kept_keys = picker(keep_index, key_rows)
    kept_values = picker(keep_index, value_rows)
    slot_place = jnp.arange(KEEP, dtype=jnp.int32) % BLOCK
    live_slots = slot_place[None, None, :] < jnp.repeat(keep_count, BLOCK, axis=2)
    source_host = jnp.repeat(jnp.arange(host_total, dtype=jnp.int32), KEEP)
    causal = jnp.arange(TOK_DEV, dtype=jnp.int32)[:, None] >= jnp.arange(TOK_DEV, dtype=jnp.int32)[None, :]

    def one_head(pair_index):
        own_host = pair_index // KVH
        kv_head = pair_index % KVH
        query_block = query_rows[own_host, :, kv_head].astype(jnp.float32)
        key_all = jnp.concatenate([key_rows[0, :ANCHOR, kv_head], kept_keys[:, kv_head].reshape(-1, HD), key_rows[own_host, :, kv_head]], axis=0).astype(jnp.float32)
        value_all = jnp.concatenate([value_rows[0, :ANCHOR, kv_head], kept_values[:, kv_head].reshape(-1, HD), value_rows[own_host, :, kv_head]], axis=0).astype(jnp.float32)
        pass_live = (source_host < own_host) & live_slots[:, kv_head].reshape(-1)
        allowed = jnp.concatenate([jnp.broadcast_to(own_host > 0, (TOK_DEV, ANCHOR)), jnp.broadcast_to(pass_live[None, :], (TOK_DEV, host_total * KEEP)), causal], axis=1)
        scores = jnp.einsum('igd,nd->gin', query_block, key_all) * score_scale
        scores = jnp.where(allowed[None], scores, -jnp.inf)
        row_max = jnp.max(scores, axis=2, keepdims=True)
        weights = jnp.exp(scores - row_max)
        weight_sum = jnp.sum(weights, axis=2)
        rounded = lax.optimization_barrier(weights.astype(jnp.bfloat16)).astype(jnp.float32)
        blended = jnp.einsum('gin,nd->gid', rounded, value_all) / weight_sum[..., None]
        return blended.astype(jnp.bfloat16)

    heads_out = lax.map(one_head, jnp.arange(host_total * KVH, dtype=jnp.int32))
    heads_out = heads_out.reshape(host_total, KVH, group_size, TOK_DEV, HD)
    return heads_out.transpose(0, 3, 1, 2, 4).reshape(TOKENS, QH * HD)
```

```python
import jax
import jax.numpy as jnp
from jax import lax
from jax.experimental import pallas as pl
from jax.experimental.pallas import tpu as pltpu
from jax.sharding import Mesh, PartitionSpec as P

QH = 64
KVH = 8
HD = 128
TOK = 192
ANCHOR = 128
GROUP = QH // KVH
ROWS = GROUP * TOK
LIVE = 96
MARK = 16.0
LIMIT = 8.0
Z, X, C, T = 8, 4, 2, 8
HALF = ANCHOR
SLOT = 2 * LIVE + HALF
LIST = Z * LIVE
COLUMN = 2 * LIST + HALF
TILE = 384
NEG = -1e30
LOG2E = 1.4426950408889634
SCALE = HD ** (-0.5) * LOG2E
LIMIT_BYTES = 40 * 1024 * 1024

VM = pl.BlockSpec(memory_space=pltpu.VMEM)
SM = pl.BlockSpec(memory_space=pltpu.SMEM)


def call(kernel, out_shape, in_specs, out_specs, scratch=(), flops=0):
    return pl.pallas_call(
        kernel,
        out_shape=out_shape,
        in_specs=in_specs,
        out_specs=out_specs,
        scratch_shapes=list(scratch),
        compiler_params=pltpu.CompilerParams(vmem_limit_bytes=LIMIT_BYTES),
        cost_estimate=pl.CostEstimate(flops=flops, bytes_accessed=1 << 20, transcendentals=0),
    )


def pick_kernel(count_ref, index_ref, keys_ref, values_ref, out_ref):
    count = count_ref[0, 0, 0]
    index = index_ref[0]
    lane = lax.broadcasted_iota(jnp.int32, (1, HD), 1)
    first = jnp.sum(jnp.where(lane == 0, index, 0))
    index = jnp.where(lane < count, index, first)
    row = lax.broadcasted_iota(jnp.int32, (TOK, HD), 0)
    hot = (row == index).astype(jnp.float32).astype(jnp.bfloat16)
    contract = (((0,), (0,)), ((), ()))
    picked_keys = lax.dot_general(hot, keys_ref[...], contract, preferred_element_type=jnp.float32)
    picked_values = lax.dot_general(
        hot, values_ref[...], contract, preferred_element_type=jnp.float32
    )
    slot = lax.broadcasted_iota(jnp.int32, (HD, HD), 0)
    picked_values = jnp.where(slot < count, picked_values, MARK)
    out_ref[:LIVE] = picked_keys[:LIVE].astype(jnp.bfloat16)
    out_ref[LIVE:] = picked_values[:LIVE].astype(jnp.bfloat16)


def spread_kernel(place_ref, picked_ref, keys_ref, passed_ref, out_ref):
    even = place_ref[1] == 0
    half = jnp.where(even, keys_ref[:ANCHOR].astype(jnp.float32), passed_ref[...].astype(jnp.float32))
    half = half.astype(jnp.bfloat16)
    for to in range(Z):
        out_ref[to, : 2 * LIVE] = picked_ref[...]
        out_ref[to, 2 * LIVE :] = half


def regroup_kernel(blocks_ref, out_ref):
    for to in range(X):
        for z in range(Z):
            out_ref[to, z * LIVE : (z + 1) * LIVE] = blocks_ref[z, :LIVE]
            out_ref[to, LIST + z * LIVE : LIST + (z + 1) * LIVE] = blocks_ref[z, LIVE : 2 * LIVE]
        out_ref[to, 2 * LIST :] = blocks_ref[0, 2 * LIVE :]


def fold(tile, queries_ref, key_rows, value_rows, most_ref, total_ref, mask=None, first=False):
    at = pl.ds(tile * TILE, TILE)
    scores = lax.dot_general(
        queries_ref[at, :],
        key_rows,
        (((1,), (1,)), ((), ())),
        preferred_element_type=jnp.float32,
    )
    if mask is not None:
        scores = jnp.where(mask, scores, NEG)
    peak = jnp.max(scores, axis=1, keepdims=True)
    if first:
        most = jnp.broadcast_to(peak, (TILE, HD))
    else:
        before = most_ref[at, :]
        most = jnp.maximum(before, peak)
    weights = jnp.exp2((scores - most[:, :1]) * SCALE).astype(jnp.bfloat16)
    added = jnp.dot(weights, value_rows, preferred_element_type=jnp.float32)
    if first:
        total_ref[at, :] = added
    else:
        ratio = jnp.exp2((before - most) * SCALE)
        total_ref[at, :] = total_ref[at, :] * jnp.concatenate([ratio, ratio], axis=1) + added
    most_ref[at, :] = most


def fill(stacked, queries_ref):
    for head in range(GROUP):
        stacked[head * TOK : (head + 1) * TOK, :] = queries_ref[:, head * HD : (head + 1) * HD]


def marked(values, keep):
    ok = (values < LIMIT) & keep
    kept = jnp.where(ok, values, 0.0).astype(jnp.bfloat16)
    ones = jnp.where(ok, 1.0, 0.0).astype(jnp.bfloat16)
    return jnp.concatenate([kept, ones], axis=1)


def columns(place_ref, core, stand_in, columns_ref, stacked, most_ref, total_ref):
    own_z, own_side = place_ref[0], place_ref[2] * C + place_ref[1]
    row = lax.broadcasted_iota(jnp.int32, (LIST, HD), 0)

    def column(x, carry):
        hosts = own_z + (x * C + core < own_side).astype(jnp.int32)
        keep = row < hosts * LIVE
        key_rows = columns_ref[x, :LIST].astype(jnp.float32)
        key_rows = jnp.where(keep, key_rows, stand_in).astype(jnp.bfloat16)
        value_rows = marked(columns_ref[x, LIST : 2 * LIST].astype(jnp.float32), keep)
        for tile in range(ROWS // TILE):
            fold(tile, stacked, key_rows, value_rows, most_ref, total_ref)
        return carry

    lax.fori_loop(0, X, column, 0)


def near_kernel(place_ref, queries_ref, keys_ref, values_ref, columns_ref, most_ref, total_ref, stacked):
    fill(stacked, queries_ref)
    row = lax.broadcasted_iota(jnp.int32, (TILE, TOK), 0)
    token = jnp.where(row >= TOK, row - TOK, row)
    causal = token >= lax.broadcasted_iota(jnp.int32, (TILE, TOK), 1)
    value_rows = jnp.concatenate([values_ref[...], jnp.ones((TOK, HD), jnp.bfloat16)], axis=1)
    for tile in range(ROWS // TILE):
        fold(tile, stacked, keys_ref[...], value_rows, most_ref, total_ref, causal, True)
    stand_in = keys_ref[:1].astype(jnp.float32)
    columns(place_ref, place_ref[1], stand_in, columns_ref, stacked, most_ref, total_ref)


def far_kernel(
    place_ref, queries_ref, keys_ref, own_half_ref, columns_ref, most_in, total_in, out_ref, stacked, most_ref, total_ref
):
    fill(stacked, queries_ref)
    stand_in = keys_ref[:1].astype(jnp.float32)
    most_ref[...] = most_in[...]
    total_ref[...] = total_in[...]
    columns(place_ref, 1 - place_ref[1], stand_in, columns_ref, stacked, most_ref, total_ref)
    even = place_ref[1] == 0
    mine = own_half_ref[...].astype(jnp.float32)
    other = columns_ref[0, 2 * LIST :].astype(jnp.float32)
    row = lax.broadcasted_iota(jnp.int32, (ANCHOR, HD), 0)
    own = place_ref[0] * (X * C) + place_ref[2] * C + place_ref[1]
    keep = row < jnp.where(own > 0, ANCHOR, 0)
    key_rows = jnp.where(keep, jnp.where(even, mine, other), stand_in).astype(jnp.bfloat16)
    value_rows = marked(jnp.where(even, other, mine), keep)
    for tile in range(ROWS // TILE):
        fold(tile, stacked, key_rows, value_rows, most_ref, total_ref)
    for head in range(GROUP):
        at = pl.ds(head * TOK, TOK)
        done = total_ref[at, :HD] / total_ref[at, HD:]
        out_ref[:, head * HD : (head + 1) * HD] = done.astype(jnp.bfloat16)


def body(queries, keys, values, keep_index, keep_count):
    half = jnp.bfloat16
    place = jnp.stack(
        [lax.axis_index("z"), lax.axis_index("core"), lax.axis_index("x"), lax.axis_index("x")]
    ).astype(jnp.int32)
    passed = lax.ppermute(values[:ANCHOR], ("z", "x", "core"), [(0, 1)])
    picked = call(
        pick_kernel, jax.ShapeDtypeStruct((2 * LIVE, HD), half), [SM, VM, VM, VM], VM, flops=1 << 24
    )(keep_count, keep_index, keys, values)
    blocks = call(
        spread_kernel, jax.ShapeDtypeStruct((Z, SLOT, HD), half), [SM, VM, VM, VM], VM
    )(place, picked, keys, passed)
    blocks = lax.all_to_all(blocks, "z", 0, 0, tiled=True)
    column = call(
        regroup_kernel, jax.ShapeDtypeStruct((X, COLUMN, HD), half), [VM], VM
    )(blocks)
    column = lax.all_to_all(column, "x", 0, 0, tiled=True)
    other = lax.ppermute(column, "core", [(0, 1), (1, 0)])
    flops = 4 * ROWS * X * LIST * HD
    most, total = call(
        near_kernel,
        (
            jax.ShapeDtypeStruct((ROWS, HD), jnp.float32),
            jax.ShapeDtypeStruct((ROWS, 2 * HD), jnp.float32),
        ),
        [SM, VM, VM, VM, VM],
        (VM, VM),
        [pltpu.VMEM((ROWS, HD), half)],
        flops,
    )(place, queries, keys, values, column)
    attended = call(
        far_kernel,
        jax.ShapeDtypeStruct((TOK, GROUP * HD), half),
        [SM, VM, VM, VM, VM, VM, VM],
        VM,
        [
            pltpu.VMEM((ROWS, HD), half),
            pltpu.VMEM((ROWS, HD), jnp.float32),
            pltpu.VMEM((ROWS, 2 * HD), jnp.float32),
        ],
        flops,
    )(place, queries, keys, column[0, 2 * LIST :], other, most, total)
    return lax.all_to_all(attended, "tensor", split_axis=0, concat_axis=1, tiled=True)


def solution(mesh):
    parts = Mesh(mesh.devices.reshape(Z, X, C, T), ("z", "x", "core", "tensor"))
    hosts = ("z", "x", "core")
    placed = (
        P(hosts, "tensor"),
        P(hosts, "tensor"),
        P(hosts, "tensor"),
        P(hosts, "tensor", None),
        P(hosts, "tensor", None),
    )
    return jax.shard_map(
        body, mesh=parts, in_specs=placed, out_specs=P(hosts + ("tensor",), None), check_vma=False
    )
```

```python
import jax
import jax.numpy as jnp
from jax import lax
from jax.experimental import pallas as pl
from jax.experimental.pallas import tpu as pltpu
from jax.sharding import Mesh, PartitionSpec as P

QH = 64
KVH = 8
HD = 128
TOK = 192
ANCHOR = 128
GROUP = QH // KVH
ROWS = GROUP * TOK
LIVE = 96
MARK = 16.0
LIMIT = 8.0
Z, X, C, T = 8, 4, 2, 8
HALF = ANCHOR
SLOT = 2 * LIVE + HALF
LIST = Z * LIVE
COLUMN = 2 * LIST + HALF
PIECE = 16
TILE = 768
ONES = 8
SAFE = 2.0**100
NEG = -1e30
LOG2E = 1.4426950408889634
SCALE = HD ** (-0.5) * LOG2E
LIMIT_BYTES = 40 * 1024 * 1024

VM = pl.BlockSpec(memory_space=pltpu.VMEM)
HBM = pl.BlockSpec(memory_space=pltpu.HBM)


def call(kernel, out_shape, in_specs, out_specs, scratch=(), flops=0, limit=LIMIT_BYTES):
    return pl.pallas_call(
        kernel,
        out_shape=out_shape,
        in_specs=in_specs,
        out_specs=out_specs,
        scratch_shapes=list(scratch),
        compiler_params=pltpu.CompilerParams(vmem_limit_bytes=limit),
        cost_estimate=pl.CostEstimate(flops=flops, bytes_accessed=1 << 20, transcendentals=0),
    )


def pack_kernel(
    count_in, index_in, keys_in, values_in, passed_ref, out_ref, count_ref, index_ref, keys_ref, values_ref, sems
):
    pairs = (
        (count_in, count_ref),
        (index_in, index_ref),
        (keys_in, keys_ref),
        (values_in, values_ref),
    )
    copies = [pltpu.make_async_copy(a, b, sems.at[n]) for n, (a, b) in enumerate(pairs)]
    for copy in copies:
        copy.start()
    for copy in copies:
        copy.wait()
    count = count_ref[0, 0, 0]
    index = index_ref[0]
    lane = lax.broadcasted_iota(jnp.int32, (1, HD), 1)
    first = jnp.sum(jnp.where(lane == 0, index, 0))
    index = jnp.where(lane < count, index, first)
    row = lax.broadcasted_iota(jnp.int32, (TOK, HD), 0)
    hot = (row == index).astype(jnp.float32).astype(jnp.bfloat16)
    contract = (((0,), (0,)), ((), ()))
    picked_keys = lax.dot_general(hot, keys_ref[...], contract, preferred_element_type=jnp.float32)
    picked_values = lax.dot_general(
        hot, values_ref[...], contract, preferred_element_type=jnp.float32
    )
    slot = lax.broadcasted_iota(jnp.int32, (HD, HD), 0)
    picked_values = jnp.where(slot < count, picked_values, MARK)
    even = lax.axis_index("core") == 0
    half = jnp.where(even, keys_ref[:ANCHOR].astype(jnp.float32), passed_ref[:ANCHOR].astype(jnp.float32))
    half = half.astype(jnp.bfloat16)
    for to in range(Z):
        out_ref[to, :LIVE] = picked_keys[:LIVE].astype(jnp.bfloat16)
        out_ref[to, LIVE : 2 * LIVE] = picked_values[:LIVE].astype(jnp.bfloat16)
        out_ref[to, 2 * LIVE :] = half


def regroup_kernel(blocks_ref, out_ref):
    for to in range(X):
        for z in range(Z):
            out_ref[to, z * LIVE : (z + 1) * LIVE] = blocks_ref[z, :LIVE]
            out_ref[to, LIST + z * LIVE : LIST + (z + 1) * LIVE] = blocks_ref[z, LIVE : 2 * LIVE]
        out_ref[to, 2 * LIST :] = blocks_ref[0, 2 * LIVE :]


def score(key_rows, stacked, at):
    return lax.dot_general(
        key_rows, stacked[at, :], (((1,), (1,)), ((), ())), preferred_element_type=jnp.float32
    )


def begin(keys_ref, values_ref, stacked, most_ref, total_ref):
    key = lax.broadcasted_iota(jnp.int32, (TOK, TILE), 0)
    causal = lax.broadcasted_iota(jnp.int32, (TOK, TILE), 1) % TOK >= key
    turned = jnp.transpose(values_ref[...].astype(jnp.float32))
    value_rows = jnp.concatenate([turned, jnp.ones((ONES, TOK), jnp.float32)]).astype(jnp.bfloat16)
    for tile in range(ROWS // TILE):
        at = slice(tile * TILE, (tile + 1) * TILE)
        scores = jnp.where(causal, score(keys_ref[...], stacked, at), NEG)
        most = jnp.max(scores, axis=0, keepdims=True)
        most_ref[:, at] = jnp.broadcast_to(most, (8, TILE))
        weights = jnp.exp2((scores - most) * SCALE).astype(jnp.bfloat16)
        total_ref[:, at] = jnp.dot(value_rows, weights, preferred_element_type=jnp.float32)


def fold(key_rows, value_rows, stacked, most_ref, total_ref, online):
    for tile in range(ROWS // TILE):
        at = slice(tile * TILE, (tile + 1) * TILE)
        scores = score(key_rows, stacked, at)
        most = most_ref[:1, at]
        if online:
            before = most
            most = jnp.maximum(before, jnp.max(scores, axis=0, keepdims=True))
            most_ref[:, at] = jnp.broadcast_to(most, (8, TILE))
            total_ref[:, at] = total_ref[:, at] * jnp.exp2((before - most) * SCALE)
        weights = jnp.exp2((scores - most) * SCALE).astype(jnp.bfloat16)
        total_ref[:, at] += jnp.dot(value_rows, weights, preferred_element_type=jnp.float32)


def sound(total_ref):
    return jnp.max(jnp.where(total_ref[HD : HD + 8, :] < SAFE, 0.0, 1.0)) < 0.5


def fill(stacked, queries_ref):
    for head in range(GROUP):
        stacked[head * TOK : (head + 1) * TOK, :] = queries_ref[:, head * HD : (head + 1) * HD]


def marked(values, live):
    turned = jnp.transpose(values)
    ok = (turned < LIMIT) & (lax.broadcasted_iota(jnp.int32, turned.shape, 1) < live)
    kept = jnp.where(ok, turned, 0.0)
    return jnp.concatenate([kept, jnp.where(ok[:ONES], 1.0, 0.0)]).astype(jnp.bfloat16)


def columns(core, stand_in, columns_ref, stacked, most_ref, total_ref, online):
    own_z = lax.axis_index("z")
    own_side = lax.axis_index("x") * C + lax.axis_index("core")
    row = lax.broadcasted_iota(jnp.int32, (LIST, HD), 0)

    def column(x, carry):
        live = (own_z + (x * C + core < own_side).astype(jnp.int32)) * LIVE
        key_rows = columns_ref[x, :LIST].astype(jnp.float32)
        key_rows = jnp.where(row < live, key_rows, stand_in).astype(jnp.bfloat16)
        value_rows = marked(columns_ref[x, LIST : 2 * LIST].astype(jnp.float32), live)
        fold(key_rows, value_rows, stacked, most_ref, total_ref, online)
        return carry

    lax.fori_loop(0, X, column, 0, unroll=not online)


def near_kernel(queries_ref, keys_ref, values_ref, columns_ref, most_ref, total_ref, stacked):
    fill(stacked, queries_ref)
    stand_in = keys_ref[:1].astype(jnp.float32)

    def go(online):
        begin(keys_ref, values_ref, stacked, most_ref, total_ref)
        core = lax.axis_index("core")
        columns(core, stand_in, columns_ref, stacked, most_ref, total_ref, online)

    go(False)

    @pl.when(jnp.logical_not(sound(total_ref)))
    def _():
        go(True)


def far_kernel(queries_ref, keys_ref, mine_ref, columns_ref, most_in, total_in, out_ref, stacked, most_ref, total_ref):
    fill(stacked, queries_ref)
    stand_in = keys_ref[:1].astype(jnp.float32)
    even = lax.axis_index("core") == 0
    own = lax.axis_index("z") * (X * C) + lax.axis_index("x") * C + lax.axis_index("core")
    live = jnp.where(own > 0, ANCHOR, 0)

    def go(online):
        most_ref[...] = most_in[...]
        total_ref[...] = total_in[...]
        columns(1 - lax.axis_index("core"), stand_in, columns_ref, stacked, most_ref, total_ref, online)
        mine = mine_ref[...].astype(jnp.float32)
        other = columns_ref[0, 2 * LIST :].astype(jnp.float32)
        keep = lax.broadcasted_iota(jnp.int32, (ANCHOR, HD), 0) < live
        key_rows = jnp.where(keep, jnp.where(even, mine, other), stand_in).astype(jnp.bfloat16)
        value_rows = marked(jnp.where(even, other, mine), live)
        fold(key_rows, value_rows, stacked, most_ref, total_ref, online)

    go(False)

    @pl.when(jnp.logical_not(sound(total_ref)))
    def _():
        go(True)

    for head in range(GROUP):
        at = slice(head * TOK, (head + 1) * TOK)
        done = total_ref[:HD, at] / total_ref[HD : HD + 1, at]
        out_ref[:, head * HD : (head + 1) * HD] = jnp.transpose(done).astype(jnp.bfloat16)


def body(queries, keys, values, keep_index, keep_count):
    half = jnp.bfloat16
    passed = lax.ppermute(values, ("z", "x", "core"), [(0, 1)])
    blocks = call(
        pack_kernel,
        jax.ShapeDtypeStruct((Z, SLOT, HD), half),
        [HBM] * 4 + [VM],
        VM,
        [
            pltpu.SMEM((1, 1, 1), jnp.int32),
            pltpu.VMEM((1, 1, HD), jnp.int32),
            pltpu.VMEM((TOK, HD), half),
            pltpu.VMEM((TOK, HD), half),
            pltpu.SemaphoreType.DMA((4,)),
        ],
        1 << 24,
        60 << 20,
    )(keep_count, keep_index, keys, values, passed)
    blocks = lax.all_to_all(blocks.reshape(Z, SLOT // PIECE, PIECE, HD), "z", 0, 0, tiled=True)
    blocks = blocks.reshape(Z, SLOT, HD)
    column = call(regroup_kernel, jax.ShapeDtypeStruct((X, COLUMN, HD), half), [VM], VM)(blocks)
    column = column.reshape(X, COLUMN // PIECE, PIECE, HD)
    column = lax.all_to_all(column, "x", 0, 0, tiled=True).reshape(X, COLUMN, HD)
    other = lax.ppermute(column, "core", [(0, 1), (1, 0)])
    flops = 4 * ROWS * X * LIST * HD
    state = [pltpu.VMEM((8, ROWS), jnp.float32), pltpu.VMEM((HD + ONES, ROWS), jnp.float32)]
    most, total = call(
        near_kernel,
        tuple(jax.ShapeDtypeStruct((rows, ROWS), jnp.float32) for rows in (8, HD + ONES)),
        [VM] * 4,
        (VM, VM),
        [pltpu.VMEM((ROWS, HD), half)],
        flops,
    )(queries, keys, values, column)
    attended = call(
        far_kernel,
        jax.ShapeDtypeStruct((TOK, GROUP * HD), half),
        [VM] * 6,
        VM,
        [pltpu.VMEM((ROWS, HD), half)] + state,
        flops,
    )(queries, keys, column[0, 2 * LIST :], other, most, total)
    return lax.all_to_all(attended, "tensor", split_axis=0, concat_axis=1, tiled=True)


def solution(mesh):
    parts = Mesh(mesh.devices.reshape(Z, X, C, T), ("z", "x", "core", "tensor"))
    hosts = ("z", "x", "core")
    placed = (
        P(hosts, "tensor"),
        P(hosts, "tensor"),
        P(hosts, "tensor"),
        P(hosts, "tensor", None),
        P(hosts, "tensor", None),
    )
    return jax.shard_map(
        body, mesh=parts, in_specs=placed, out_specs=P(hosts + ("tensor",), None), check_vma=False
    )
```

```python
import jax
import jax.numpy as jnp
from jax import lax
from jax.experimental import pallas as pl
from jax.experimental.pallas import tpu as pltpu
from jax.sharding import Mesh, PartitionSpec as P

QH = 64
KVH = 8
HD = 128
TOK = 192
ANCHOR = 128
GROUP = QH // KVH
ROWS = GROUP * TOK
LIVE = 96
MARK = 16.0
LIMIT = 8.0
Z, X, C, T = 8, 4, 2, 8
SLOT = 2 * LIVE
LIST = Z * LIVE
COLUMN = 2 * LIST
LEAD = (Z * X - 1) * C
PIECE = 16
TILE = 768
ONES = 8
SAFE = 2.0**100
NEG = -1e30
LOG2E = 1.4426950408889634
SCALE = HD ** (-0.5) * LOG2E
LIMIT_BYTES = 40 * 1024 * 1024

VM = pl.BlockSpec(memory_space=pltpu.VMEM)


def call(kernel, out_shape, in_specs, out_specs, scratch=(), flops=0):
    return pl.pallas_call(
        kernel,
        out_shape=out_shape,
        in_specs=in_specs,
        out_specs=out_specs,
        scratch_shapes=list(scratch),
        compiler_params=pltpu.CompilerParams(vmem_limit_bytes=LIMIT_BYTES),
        cost_estimate=pl.CostEstimate(flops=flops, bytes_accessed=1 << 20, transcendentals=0),
    )


def lead_half(passed_keys_ref, passed_values_ref):
    even = lax.axis_index("core") == 0
    half = jnp.where(
        even,
        passed_keys_ref[:ANCHOR].astype(jnp.float32),
        passed_values_ref[:ANCHOR].astype(jnp.float32),
    )
    return half.astype(jnp.bfloat16)


def pack_kernel(picks_ref, pair_ref, passed_keys_ref, passed_values_ref, out_ref):
    slots, count = picks_ref[0, :, :HD], picks_ref[0, :, HD : HD + 1]
    lane = lax.broadcasted_iota(jnp.int32, (1, HD), 1)
    picks = jnp.where(lane < count, slots, slots[:, :1])
    row = lax.broadcasted_iota(jnp.int32, (TOK, HD), 0)
    contract = (((0,), (0,)), ((), ()))
    hot = (row == picks).astype(jnp.float32).astype(jnp.bfloat16)
    picked = lax.dot_general(hot, pair_ref[...], contract, preferred_element_type=jnp.float32)
    slot = lax.broadcasted_iota(jnp.int32, (HD, HD), 0)
    picked_keys = picked[:LIVE, :HD].astype(jnp.bfloat16)
    picked_values = jnp.where(slot < count, picked[:, HD:], MARK)[:LIVE].astype(jnp.bfloat16)
    for to in range(Z):
        out_ref[to, :LIVE] = picked_keys
        out_ref[to, LIVE:] = picked_values

    @pl.when((lax.axis_index("z") == Z - 1) & (lax.axis_index("x") == X - 1))
    def _():
        half = lead_half(passed_keys_ref, passed_values_ref)
        for to in range(Z - 1):
            out_ref[to, :ANCHOR] = half


def regroup_kernel(blocks_ref, passed_keys_ref, passed_values_ref, out_ref):
    for to in range(X):
        for z in range(Z):
            out_ref[to, z * LIVE : (z + 1) * LIVE] = blocks_ref[z, :LIVE]
            out_ref[to, LIST + z * LIVE : LIST + (z + 1) * LIVE] = blocks_ref[z, LIVE:]
    z, last = lax.axis_index("z"), lax.axis_index("x") == X - 1

    def put(to, half):
        at = pl.multiple_of(z * LIVE, 32)
        out_ref[to, pl.ds(at, LIVE)] = half[:LIVE]
        out_ref[to, pl.ds(pl.multiple_of(LIST + at, 32), ANCHOR - LIVE)] = half[LIVE:]

    @pl.when(last & (z < Z - 1))
    def _():
        for to in range(X - 1):
            put(to, blocks_ref[Z - 1, :ANCHOR])

    @pl.when(last & (z == Z - 1))
    def _():
        half = lead_half(passed_keys_ref, passed_values_ref)
        for to in range(X - 1):
            put(to, half)

        @pl.when(lax.axis_index("core") == C - 1)
        def _():
            put(X - 1, half)


def anchor_half(columns_ref):
    place = jnp.where(lax.axis_index("x") == X - 1, Z - 1, lax.axis_index("z"))
    at = pl.multiple_of(place * LIVE, 32)
    low = columns_ref[X - 1, pl.ds(at, LIVE)].astype(jnp.float32)
    high = columns_ref[X - 1, pl.ds(pl.multiple_of(LIST + at, 32), ANCHOR - LIVE)]
    return jnp.concatenate([low, high.astype(jnp.float32)])


def score(key_rows, stacked, at):
    return lax.dot_general(
        key_rows, stacked[at, :], (((1,), (1,)), ((), ())), preferred_element_type=jnp.float32
    )


def begin(keys_ref, values_ref, stacked, most_ref, total_ref):
    key = lax.broadcasted_iota(jnp.int32, (TOK, TILE), 0)
    causal = lax.broadcasted_iota(jnp.int32, (1, TILE), 1) % TOK >= key
    turned = jnp.transpose(values_ref[...].astype(jnp.float32))
    value_rows = jnp.concatenate([turned, jnp.ones((ONES, TOK), jnp.float32)]).astype(jnp.bfloat16)
    for tile in range(ROWS // TILE):
        at = slice(tile * TILE, (tile + 1) * TILE)
        scores = jnp.where(causal, score(keys_ref[...], stacked, at), NEG)
        most = jnp.max(scores, axis=0, keepdims=True)
        most_ref[:, at] = jnp.broadcast_to(most, (8, TILE))
        weights = jnp.exp2((scores - most) * SCALE).astype(jnp.bfloat16)
        total_ref[:, at] = jnp.dot(value_rows, weights, preferred_element_type=jnp.float32)


def fold(key_rows, value_rows, stacked, most_ref, total_ref, source, online):
    for tile in range(ROWS // TILE):
        at = slice(tile * TILE, (tile + 1) * TILE)
        scores = score(key_rows, stacked, at)
        most = most_ref[:1, at]
        total = source[:, at]
        if online:
            before = most
            most = jnp.maximum(before, jnp.max(scores, axis=0, keepdims=True))
            most_ref[:, at] = jnp.broadcast_to(most, (8, TILE))
            total = total * jnp.exp2((before - most) * SCALE)
        weights = jnp.exp2((scores - most) * SCALE).astype(jnp.bfloat16)
        total_ref[:, at] = total + jnp.dot(value_rows, weights, preferred_element_type=jnp.float32)


def sound(total_ref):
    return jnp.max(jnp.where(total_ref[HD : HD + 8, :] < SAFE, 0.0, 1.0)) < 0.5


def fill(stacked, queries_ref):
    for head in range(GROUP):
        stacked[head * TOK : (head + 1) * TOK, :] = queries_ref[:, head * HD : (head + 1) * HD]


def marked(values, live):
    turned = jnp.transpose(values)
    ok = (turned < LIMIT) & (lax.broadcasted_iota(jnp.int32, turned.shape, 1) < live)
    kept = jnp.where(ok, turned, 0.0)
    return jnp.concatenate([kept, jnp.where(ok[:ONES], 1.0, 0.0)]).astype(jnp.bfloat16)


def columns(core, stand_in, columns_ref, stacked, most_ref, total_ref, online):
    own_z = lax.axis_index("z")
    own_side = lax.axis_index("x") * C + lax.axis_index("core")
    row = lax.broadcasted_iota(jnp.int32, (LIST, HD), 0)

    def column(x, carry):
        live = (own_z + (x * C + core < own_side).astype(jnp.int32)) * LIVE
        key_rows = columns_ref[x, :LIST].astype(jnp.float32)
        key_rows = jnp.where(row < live, key_rows, stand_in).astype(jnp.bfloat16)
        value_rows = marked(columns_ref[x, LIST : 2 * LIST].astype(jnp.float32), live)
        fold(key_rows, value_rows, stacked, most_ref, total_ref, total_ref, online)
        return carry

    lax.fori_loop(0, X, column, 0, unroll=not online)


def near_kernel(queries_ref, keys_ref, values_ref, columns_ref, most_ref, total_ref, stacked):
    fill(stacked, queries_ref)
    stand_in = keys_ref[:1].astype(jnp.float32)

    def go(online):
        begin(keys_ref, values_ref, stacked, most_ref, total_ref)
        core = lax.axis_index("core")
        columns(core, stand_in, columns_ref, stacked, most_ref, total_ref, online)

    go(False)

    @pl.when(jnp.logical_not(sound(total_ref)))
    def _():
        go(True)


def far_kernel(
    stacked,
    keys_ref,
    passed_keys_ref,
    passed_values_ref,
    extra_keys_ref,
    near_ref,
    columns_ref,
    most_in,
    total_in,
    out_ref,
    most_ref,
    total_ref,
):
    stand_in = keys_ref[:1].astype(jnp.float32)
    even = lax.axis_index("core") == 0
    own = lax.axis_index("z") * (X * C) + lax.axis_index("x") * C + lax.axis_index("core")
    live = jnp.where(own > 0, ANCHOR, 0)

    def go(online):
        most_ref[...] = most_in[...]
        mine, other = anchor_half(near_ref), anchor_half(columns_ref)
        lead_keys = jnp.where(
            even,
            passed_keys_ref[:ANCHOR].astype(jnp.float32),
            extra_keys_ref[:ANCHOR].astype(jnp.float32),
        )
        anchor_keys = jnp.where(own >= LEAD, lead_keys, jnp.where(even, mine, other))
        anchor_values = jnp.where(even, other, mine)
        anchor_values = jnp.where(
            own == LEAD + 1, passed_values_ref[:ANCHOR].astype(jnp.float32), anchor_values
        )
        keep = lax.broadcasted_iota(jnp.int32, (ANCHOR, HD), 0) < live
        key_rows = jnp.where(keep, anchor_keys, stand_in).astype(jnp.bfloat16)
        value_rows = marked(anchor_values, live)
        fold(key_rows, value_rows, stacked, most_ref, total_ref, total_in, online)
        columns(1 - lax.axis_index("core"), stand_in, columns_ref, stacked, most_ref, total_ref, online)

    go(False)

    @pl.when(jnp.logical_not(sound(total_ref)))
    def _():
        go(True)

    for head in range(GROUP):
        at = slice(head * TOK, (head + 1) * TOK)
        done = total_ref[:HD, at] * (1.0 / total_ref[HD : HD + 1, at])
        out_ref[:, head * HD : (head + 1) * HD] = jnp.transpose(done).astype(jnp.bfloat16)


def body(queries, keys, values, keep_index, keep_count):
    half = jnp.bfloat16
    hosts = ("z", "x", "core")
    passed_keys = lax.ppermute(keys, hosts, [(0, LEAD)])
    passed_values = lax.ppermute(values, hosts, [(0, LEAD + 1)])
    extra_keys = lax.ppermute(keys, hosts, [(0, LEAD + 1)])
    picks = jnp.concatenate([keep_index, keep_count], axis=2)
    pair = jnp.concatenate([keys, values], axis=1)
    blocks = call(
        pack_kernel, jax.ShapeDtypeStruct((Z, SLOT, HD), half), [VM] * 4, VM, flops=1 << 24
    )(picks, pair, passed_keys, passed_values)
    blocks = lax.all_to_all(blocks.reshape(Z, SLOT // PIECE, PIECE, HD), "z", 0, 0, tiled=True)
    blocks = blocks.reshape(Z, SLOT, HD)
    column = call(regroup_kernel, jax.ShapeDtypeStruct((X, COLUMN, HD), half), [VM] * 3, VM)(
        blocks, passed_keys, passed_values
    )
    column = column.reshape(X, COLUMN // PIECE, PIECE, HD)
    column = lax.all_to_all(column, "x", 0, 0, tiled=True).reshape(X, COLUMN, HD)
    other = lax.ppermute(column, "core", [(0, 1), (1, 0)])
    flops = 4 * ROWS * X * LIST * HD
    state = [pltpu.VMEM((8, ROWS), jnp.float32), pltpu.VMEM((HD + ONES, ROWS), jnp.float32)]
    most, total, stacked = call(
        near_kernel,
        tuple(jax.ShapeDtypeStruct((rows, ROWS), jnp.float32) for rows in (8, HD + ONES))
        + (jax.ShapeDtypeStruct((ROWS, HD), half),),
        [VM] * 4,
        (VM,) * 3,
        flops=flops,
    )(queries, keys, values, column)
    attended = call(
        far_kernel,
        jax.ShapeDtypeStruct((TOK, GROUP * HD), half),
        [VM] * 9,
        VM,
        state,
        flops,
    )(stacked, keys, passed_keys, passed_values, extra_keys, column, other, most, total)
    return lax.all_to_all(attended, "tensor", split_axis=0, concat_axis=1, tiled=True)


def solution(mesh):
    parts = Mesh(mesh.devices.reshape(Z, X, C, T), ("z", "x", "core", "tensor"))
    hosts = ("z", "x", "core")
    placed = (
        P(hosts, "tensor"),
        P(hosts, "tensor"),
        P(hosts, "tensor"),
        P(hosts, "tensor", None),
        P(hosts, "tensor", None),
    )
    return jax.shard_map(
        body, mesh=parts, in_specs=placed, out_specs=P(hosts + ("tensor",), None), check_vma=False
    )
```

```python
import jax
import jax.numpy as jnp
from jax import lax
from jax.experimental import pallas as pl
from jax.experimental.pallas import tpu as pltpu
from jax.sharding import Mesh, PartitionSpec as P

QH = 64
KVH = 8
HD = 128
TOK = 192
ANCHOR = 128
GROUP = QH // KVH
ROWS = GROUP * TOK
LIVE = 96
MARK = 16.0
LIMIT = 8.0
Z, X, C, T = 8, 4, 2, 8
SLOT = 2 * LIVE
LIST = Z * LIVE
COLUMN = 2 * LIST
LEAD = (Z * X - 1) * C
PIECE = 16
TILE = 768
ONES = 8
SAFE = 2.0**100
NEG = -1e30
LOG2E = 1.4426950408889634
SCALE = HD ** (-0.5) * LOG2E
LIMIT_BYTES = 40 * 1024 * 1024

VM = pl.BlockSpec(memory_space=pltpu.VMEM)


def call(kernel, out_shape, in_specs, out_specs, scratch=(), flops=0):
    return pl.pallas_call(
        kernel,
        out_shape=out_shape,
        in_specs=in_specs,
        out_specs=out_specs,
        scratch_shapes=list(scratch),
        compiler_params=pltpu.CompilerParams(vmem_limit_bytes=LIMIT_BYTES),
        cost_estimate=pl.CostEstimate(flops=flops, bytes_accessed=1 << 20, transcendentals=0),
    )


def lead_half(passed_keys_ref, passed_values_ref):
    even = lax.axis_index("core") == 0
    half = jnp.where(
        even,
        passed_keys_ref[:ANCHOR].astype(jnp.float32),
        passed_values_ref[:ANCHOR].astype(jnp.float32),
    )
    return half.astype(jnp.bfloat16)


def pack_kernel(picks_ref, pair_ref, passed_keys_ref, passed_values_ref, out_ref):
    slots, count = picks_ref[0, :, :HD], picks_ref[0, :, HD : HD + 1]
    lane = lax.broadcasted_iota(jnp.int32, (1, HD), 1)
    picks = jnp.where(lane < count, slots, slots[:, :1])
    row = lax.broadcasted_iota(jnp.int32, (TOK, HD), 0)
    contract = (((0,), (0,)), ((), ()))
    hot = (row == picks).astype(jnp.float32).astype(jnp.bfloat16)
    picked = lax.dot_general(hot, pair_ref[...], contract, preferred_element_type=jnp.float32)
    slot = lax.broadcasted_iota(jnp.int32, (HD, HD), 0)
    picked_keys = picked[:LIVE, :HD].astype(jnp.bfloat16)
    picked_values = jnp.where(slot < count, picked[:, HD:], MARK)[:LIVE].astype(jnp.bfloat16)
    for to in range(Z):
        out_ref[to, :LIVE] = picked_keys
        out_ref[to, LIVE:] = picked_values

    @pl.when((lax.axis_index("z") == Z - 1) & (lax.axis_index("x") == X - 1))
    def _():
        half = lead_half(passed_keys_ref, passed_values_ref)
        for to in range(Z - 1):
            out_ref[to, :ANCHOR] = half


def regroup_kernel(blocks_ref, passed_keys_ref, passed_values_ref, out_ref):
    for to in range(X):
        for z in range(Z):
            out_ref[to, z * LIVE : (z + 1) * LIVE] = blocks_ref[z, :LIVE]
            out_ref[to, LIST + z * LIVE : LIST + (z + 1) * LIVE] = blocks_ref[z, LIVE:]
    z, last = lax.axis_index("z"), lax.axis_index("x") == X - 1

    def put(to, half):
        at = pl.multiple_of(z * LIVE, 32)
        out_ref[to, pl.ds(at, LIVE)] = half[:LIVE]
        out_ref[to, pl.ds(pl.multiple_of(LIST + at, 32), ANCHOR - LIVE)] = half[LIVE:]

    @pl.when(last & (z < Z - 1))
    def _():
        for to in range(X - 1):
            put(to, blocks_ref[Z - 1, :ANCHOR])

    @pl.when(last & (z == Z - 1))
    def _():
        half = lead_half(passed_keys_ref, passed_values_ref)
        for to in range(X - 1):
            put(to, half)

        @pl.when(lax.axis_index("core") == C - 1)
        def _():
            put(X - 1, half)


def anchor_half(columns_ref):
    place = jnp.where(lax.axis_index("x") == X - 1, Z - 1, lax.axis_index("z"))
    at = pl.multiple_of(place * LIVE, 32)
    at = pl.multiple_of((X - 1) * COLUMN + at, 32)
    low = columns_ref[pl.ds(at, LIVE)].astype(jnp.float32)
    high = columns_ref[pl.ds(pl.multiple_of(LIST + at, 32), ANCHOR - LIVE)]
    return jnp.concatenate([low, high.astype(jnp.float32)])


def score(key_rows, stacked, at):
    return lax.dot_general(
        key_rows, stacked[at, :], (((1,), (1,)), ((), ())), preferred_element_type=jnp.float32
    )


def begin(keys_ref, values_ref, stacked, most_ref, total_ref):
    key = lax.broadcasted_iota(jnp.int32, (TOK, TILE), 0)
    causal = lax.broadcasted_iota(jnp.int32, (1, TILE), 1) % TOK >= key
    turned = jnp.transpose(values_ref[...].astype(jnp.float32))
    value_rows = jnp.concatenate([turned, jnp.ones((ONES, TOK), jnp.float32)]).astype(jnp.bfloat16)
    for tile in range(ROWS // TILE):
        at = slice(tile * TILE, (tile + 1) * TILE)
        scores = jnp.where(causal, score(keys_ref[...], stacked, at), NEG)
        most = jnp.max(scores, axis=0, keepdims=True)
        most_ref[:, at] = jnp.broadcast_to(most, (8, TILE))
        weights = jnp.exp2((scores - most) * SCALE).astype(jnp.bfloat16)
        total_ref[:, at] = jnp.dot(value_rows, weights, preferred_element_type=jnp.float32)


def fold(key_rows, value_rows, stacked, most_ref, total_ref, source, online):
    for tile in range(ROWS // TILE):
        at = slice(tile * TILE, (tile + 1) * TILE)
        scores = score(key_rows, stacked, at)
        most = most_ref[:1, at]
        total = source[:, at]
        if online:
            before = most
            most = jnp.maximum(before, jnp.max(scores, axis=0, keepdims=True))
            most_ref[:, at] = jnp.broadcast_to(most, (8, TILE))
            total = total * jnp.exp2((before - most) * SCALE)
        weights = jnp.exp2((scores - most) * SCALE).astype(jnp.bfloat16)
        total_ref[:, at] = total + jnp.dot(value_rows, weights, preferred_element_type=jnp.float32)


def sound(total_ref):
    return jnp.max(jnp.where(total_ref[HD : HD + 8, :] < SAFE, 0.0, 1.0)) < 0.5


def fill(stacked, queries_ref):
    for head in range(GROUP):
        stacked[head * TOK : (head + 1) * TOK, :] = queries_ref[:, head * HD : (head + 1) * HD]


def marked(values, live):
    turned = jnp.transpose(values)
    ok = (turned < LIMIT) & (lax.broadcasted_iota(jnp.int32, turned.shape, 1) < live)
    kept = jnp.where(ok, turned, 0.0)
    return jnp.concatenate([kept, jnp.where(ok[:ONES], 1.0, 0.0)]).astype(jnp.bfloat16)


def columns(core, stand_in, columns_ref, stacked, most_ref, total_ref, online):
    own_z = lax.axis_index("z")
    own_side = lax.axis_index("x") * C + lax.axis_index("core")
    row = lax.broadcasted_iota(jnp.int32, (LIST, HD), 0)

    def column(x, carry):
        live = (own_z + (x * C + core < own_side).astype(jnp.int32)) * LIVE
        at = pl.multiple_of(x * COLUMN, 32)
        key_rows = columns_ref[pl.ds(at, LIST)].astype(jnp.float32)
        key_rows = jnp.where(row < live, key_rows, stand_in).astype(jnp.bfloat16)
        value_rows = columns_ref[pl.ds(pl.multiple_of(at + LIST, 32), LIST)].astype(jnp.float32)
        value_rows = marked(value_rows, live)
        fold(key_rows, value_rows, stacked, most_ref, total_ref, total_ref, online)
        return carry

    lax.fori_loop(0, X, column, 0, unroll=not online)


def near_kernel(queries_ref, keys_ref, values_ref, columns_ref, most_ref, total_ref, stacked):
    fill(stacked, queries_ref)
    stand_in = keys_ref[:1].astype(jnp.float32)

    def go(online):
        begin(keys_ref, values_ref, stacked, most_ref, total_ref)
        core = lax.axis_index("core")
        columns(core, stand_in, columns_ref, stacked, most_ref, total_ref, online)

    go(False)

    @pl.when(jnp.logical_not(sound(total_ref)))
    def _():
        go(True)


def far_kernel(
    stacked,
    keys_ref,
    passed_keys_ref,
    passed_values_ref,
    near_ref,
    columns_ref,
    most_in,
    total_in,
    out_ref,
    most_ref,
    total_ref,
):
    stand_in = keys_ref[:1].astype(jnp.float32)
    even = lax.axis_index("core") == 0
    own = lax.axis_index("z") * (X * C) + lax.axis_index("x") * C + lax.axis_index("core")
    live = jnp.where(own > 0, ANCHOR, 0)

    def go(online):
        most_ref[...] = most_in[...]
        mine, other = anchor_half(near_ref), anchor_half(columns_ref)
        lead_keys = jnp.where(
            even,
            passed_keys_ref[:ANCHOR].astype(jnp.float32),
            columns_ref[X * COLUMN : X * COLUMN + ANCHOR].astype(jnp.float32),
        )
        anchor_keys = jnp.where(own >= LEAD, lead_keys, jnp.where(even, mine, other))
        anchor_values = jnp.where(even, other, mine)
        anchor_values = jnp.where(
            own == LEAD + 1, passed_values_ref[:ANCHOR].astype(jnp.float32), anchor_values
        )
        keep = lax.broadcasted_iota(jnp.int32, (ANCHOR, HD), 0) < live
        key_rows = jnp.where(keep, anchor_keys, stand_in).astype(jnp.bfloat16)
        value_rows = marked(anchor_values, live)
        fold(key_rows, value_rows, stacked, most_ref, total_ref, total_in, online)
        columns(1 - lax.axis_index("core"), stand_in, columns_ref, stacked, most_ref, total_ref, online)

    go(False)

    @pl.when(jnp.logical_not(sound(total_ref)))
    def _():
        go(True)

    for head in range(GROUP):
        at = slice(head * TOK, (head + 1) * TOK)
        done = total_ref[:HD, at] * (1.0 / total_ref[HD : HD + 1, at])
        out_ref[:, head * HD : (head + 1) * HD] = jnp.transpose(done).astype(jnp.bfloat16)


def body(queries, keys, values, keep_index, keep_count):
    half = jnp.bfloat16
    hosts = ("z", "x", "core")
    passed_keys = lax.ppermute(keys, hosts, [(0, LEAD)])
    passed_values = lax.ppermute(values, hosts, [(0, LEAD + 1)])
    picks = jnp.concatenate([keep_index, keep_count], axis=2)
    pair = jnp.concatenate([keys, values], axis=1)
    blocks = call(
        pack_kernel, jax.ShapeDtypeStruct((Z, SLOT, HD), half), [VM] * 4, VM, flops=1 << 24
    )(picks, pair, passed_keys, passed_values)
    blocks = lax.all_to_all(blocks.reshape(Z, SLOT // PIECE, PIECE, HD), "z", 0, 0, tiled=True)
    blocks = blocks.reshape(Z, SLOT, HD)
    column = call(regroup_kernel, jax.ShapeDtypeStruct((X, COLUMN, HD), half), [VM] * 3, VM)(
        blocks, passed_keys, passed_values
    )
    column = column.reshape(X, COLUMN // PIECE, PIECE, HD)
    column = lax.all_to_all(column, "x", 0, 0, tiled=True)
    column = jnp.concatenate([column.reshape(X * COLUMN, HD), passed_keys])
    other = lax.ppermute(column, "core", [(0, 1), (1, 0)])
    flops = 4 * ROWS * X * LIST * HD
    state = [pltpu.VMEM((8, ROWS), jnp.float32), pltpu.VMEM((HD + ONES, ROWS), jnp.float32)]
    most, total, stacked = call(
        near_kernel,
        tuple(jax.ShapeDtypeStruct((rows, ROWS), jnp.float32) for rows in (8, HD + ONES))
        + (jax.ShapeDtypeStruct((ROWS, HD), half),),
        [VM] * 4,
        (VM,) * 3,
        flops=flops,
    )(queries, keys, values, column)
    attended = call(
        far_kernel,
        jax.ShapeDtypeStruct((TOK, GROUP * HD), half),
        [VM] * 8,
        VM,
        state,
        flops,
    )(stacked, keys, passed_keys, passed_values, column, other, most, total)
    return lax.all_to_all(attended, "tensor", split_axis=0, concat_axis=1, tiled=True)


def solution(mesh):
    parts = Mesh(mesh.devices.reshape(Z, X, C, T), ("z", "x", "core", "tensor"))
    hosts = ("z", "x", "core")
    placed = (
        P(hosts, "tensor"),
        P(hosts, "tensor"),
        P(hosts, "tensor"),
        P(hosts, "tensor", None),
        P(hosts, "tensor", None),
    )
    return jax.shard_map(
        body, mesh=parts, in_specs=placed, out_specs=P(hosts + ("tensor",), None), check_vma=False
    )
```
